256 devices in a mesh: tensor: 8 (over z), dp: 32 (over x, y, core).
Axes of the slice: x: 4, y: 4, z: 8, core: 2. Of those that a mesh axis runs over, the one named last changes fastest.
Arguments:
- grads: bfloat16 [32, 4096, 2048], P('dp', 'tensor'), may hold values from -6 to 6
- errors: bfloat16 [32, 4096, 2048], P('dp', 'tensor'), may hold values from -4 to 4
- basis: float32 [2048, 64], replicated, may hold values from -6 to 6
- weight: float32 [4096, 2048], P(('tensor', 'dp')), may hold values from -6 to 6
- moment: float32 [4096, 2048], P(('tensor', 'dp')), may hold values from -0.125 to 0.125
- second: float32 [4096, 2048], P(('tensor', 'dp')), may hold values from 0.0002 to 0.05
Outputs:
- new_errors: bfloat16 [32, 4096, 2048], P('dp', 'tensor')
- basis_next: float32 [2048, 64], replicated
- weight_next: float32 [4096, 2048], P(('tensor', 'dp'))
- moment_next: float32 [4096, 2048], P(('tensor', 'dp'))
- second_next: float32 [4096, 2048], P(('tensor', 'dp'))
The draws below stay inside these ranges and needn't reach their ends.
All inputs are finite; a program needn't handle non-finite values.
Results may differ from the reference program's by a relative error of at most 0.001.
Values sent between devices are 32-bit elements; how exact they have to be, the bound alone decides.
A program may use at most 64 MiB of HBM per device.

```python
import math
import jax
import jax.numpy as jnp
from jax import lax

D = 2048
RANK = 64
ROWS = 4096
N_DP = 32


def level_of(key, shape, pieces, low, top_value):
    loudness, own = 1.0, jax.random.fold_in(key, 6)
    for position, shards_of in pieces:
        draws = jnp.exp(jax.random.uniform(jax.random.fold_in(own, position), (shards_of,), jnp.float32, low / len(pieces), top_value / len(pieces)))
        loudness = loudness * jnp.repeat(draws, shape[position] // shards_of).reshape([-1 if axis == position else 1 for axis in range(len(shape))])
    return loudness


def gaussian(own_key, extent, scale, bound, pieces=(), dtype=jnp.bfloat16):
    factor_of = level_of(own_key, extent, pieces, -0.22, 0.18) if pieces else 1.0
    entries = jax.random.normal(own_key, extent, jnp.float32) * scale * factor_of
    return jnp.minimum(jnp.maximum(entries, -bound), bound).astype(dtype)


def setup_inputs(seed: int = 0) -> dict:
    key_of = jax.random.split(jax.random.key(seed), 7)
    grads = gaussian(key_of[0], (N_DP, ROWS, D), 1.0, 6.0, ((0, 32), (1, 8)))
    errors = gaussian(key_of[1], (N_DP, ROWS, D), 0.5, 4.0, ((0, 32), (1, 8)))
    basis = gaussian(key_of[2], (D, RANK), 1.0, 6.0, (), jnp.float32)
    weight = gaussian(key_of[3], (ROWS, D), 1.0, 6.0, ((0, 256),), jnp.float32)
    moment = gaussian(key_of[4], (ROWS, D), (ROWS * N_DP // RANK) ** -0.5, 0.125, ((0, 256),), jnp.float32)
    second = jnp.clip(jnp.exp(math.log(0.05) - 5.521461 * jax.random.uniform(key_of[5], (ROWS, D), jnp.float32) ** level_of(key_of[5], (ROWS, D), ((0, 256),), -0.2, 0.2)), 0.0002, 0.05)
    return dict(grads=grads, errors=errors, basis=basis, weight=weight, moment=moment, second=second)


beta_first = 0.9
beta_second = 0.95
step_size = 0.1
adam_eps = 1e-08
corr_first = 1.0 - 0.9 ** 10
corr_second = 1.0 - 0.95 ** 10

def reference(grads, errors, basis, weight, moment, second):
    highest = lax.Precision.HIGHEST

    def left_term(carry, pair):
        merged = pair[0].astype(jnp.float32) + pair[1].astype(jnp.float32)
        return (carry + jnp.dot(merged.astype(jnp.float32), basis.astype(jnp.float32), precision=highest, preferred_element_type=jnp.float32), None)
    columns, _ = lax.scan(left_term, jnp.zeros((ROWS, RANK), jnp.float32), (grads, errors))
    gram = lax.dot_general(columns.astype(jnp.float32), columns.astype(jnp.float32), (((0,), (0,)), ((), ())), precision=highest, preferred_element_type=jnp.float32)
    factor = jnp.linalg.cholesky(gram)
    ortho = lax.linalg.triangular_solve(factor, columns, left_side=False, lower=True, transpose_a=True)

    def right_term(carry, pair):
        merged = pair[0].astype(jnp.float32) + pair[1].astype(jnp.float32)
        term = lax.dot_general(merged.astype(jnp.float32), ortho.astype(jnp.float32), (((0,), (0,)), ((), ())), precision=highest, preferred_element_type=jnp.float32)
        return (carry + term, None)
    qsum, _ = lax.scan(right_term, jnp.zeros((D, RANK), jnp.float32), (grads, errors))
    basis_next = qsum / N_DP
    approx = lax.dot_general(ortho.astype(jnp.float32), basis_next.astype(jnp.float32), (((1,), (1,)), ((), ())), precision=highest, preferred_element_type=jnp.float32)

    def residue(pair):
        merged = pair[0].astype(jnp.float32) + pair[1].astype(jnp.float32)
        return (merged - approx).astype(jnp.bfloat16)
    new_errors = lax.map(residue, (grads, errors))
    moment_next = beta_first * moment + (1.0 - beta_first) * approx
    second_next = beta_second * second + (1.0 - beta_second) * approx * approx
    weight_next = weight - step_size * (moment_next / corr_first) / (jnp.sqrt(second_next / corr_second) + adam_eps)
    return (new_errors, basis_next, weight_next, moment_next, second_next)
```

```python
import jax
import jax.numpy as jnp
from jax import lax
from jax.experimental import pallas as pl
from jax.experimental.pallas import tpu as pltpu
from jax.sharding import PartitionSpec as P

beta_first = 0.9
beta_second = 0.95
step_size = 0.1
adam_eps = 1e-08
corr_first = 1.0 - 0.9**10
corr_second = 1.0 - 0.95**10

MESH = pl.DeviceIdType.MESH
VMEM = pltpu.VMEM
f32, bf16 = jnp.float32, jnp.bfloat16
D, RANK, HID, HALF = 2048, 64, 512, 256
NX, NY, NZ = 4, 4, 8
NN = (((1,), (0,)), ((), ()))
NT = (((1,), (1,)), ((), ()))
TN = (((0,), (0,)), ((), ()))
HIGH = lax.Precision.HIGHEST


def split3(v):
    hi = v.astype(bf16)
    rest = v - hi.astype(f32)
    mid = rest.astype(bf16)
    lo = (rest - mid.astype(f32)).astype(bf16)
    return hi, mid, lo


def split2(v):
    hi = v.astype(bf16)
    return hi, (v - hi.astype(f32)).astype(bf16)


def dot(a, b, dims=NN):
    return lax.dot_general(a, b, dims, preferred_element_type=f32)


def fold(v):
    return v[0:RANK] + v[RANK : 2 * RANK] + v[2 * RANK : 3 * RANK]


def eliminate(a, start, stop):
    rows = lax.broadcasted_iota(jnp.int32, (RANK, 2 * RANK), 0)
    lanes = lax.broadcasted_iota(jnp.int32, (RANK, 2 * RANK), 1)

    def step(k, a):
        row = jnp.sum(jnp.where(rows == k, a, 0.0), axis=0, keepdims=True)
        col = jnp.sum(jnp.where(lanes == k, a, 0.0), axis=1, keepdims=True)
        pivot = jnp.sum(jnp.where(lanes[0:1] == k, row, 0.0), axis=1, keepdims=True)
        root = lax.sqrt(pivot)
        row = row / root
        below = a - (col / root) * row
        return jnp.where(rows > k, below, jnp.where(rows == k, row, a))

    return lax.fori_loop(start, stop, step, a)


def exchange_kernel(
    g_hbm, e_hbm, b_hbm, bn_ref, op_ref,
    g, e, b, own_part, sib_part, one, two, c_t, r_all, r_sib, rbuf, zbuf, gram_send, gbuf, tb, aug,
    in_sem, core_s, core_r, one_s, one_r, two_s, two_r, rc_s, rc_r, xy_s, xy_r, z_s, z_r, gr_s, gr_r, ag_s, ag_r, fw_s, fw_r,
):
    t = lax.axis_index("tensor")
    d = lax.axis_index("dp")
    x, y, c = d // 8, (d // 2) % NY, d % 2
    oc = 1 - c
    chip = x * NY + y

    def dev(tt, xx, yy, cc):
        return (tt, (xx * NY + yy) * 2 + cc)

    sib = dev(t, x, y, oc)

    def plane(dx, dy):
        return (x + dx) % NX, (y + dy) % NY

    def send(src, dst, ss, rs, to):
        pltpu.make_async_remote_copy(
            src_ref=src, dst_ref=dst, send_sem=ss, recv_sem=rs, device_id=to, device_id_type=MESH
        ).start()

    def got(ref, rs):
        pltpu.make_async_remote_copy(
            src_ref=ref, dst_ref=ref, send_sem=core_s, recv_sem=rs, device_id=sib, device_id_type=MESH
        ).wait_recv()

    def sent(ref, ss):
        pltpu.make_async_remote_copy(
            src_ref=ref, dst_ref=ref, send_sem=ss, recv_sem=core_r, device_id=sib, device_id_type=MESH
        ).wait_send()

    b_in = pltpu.make_async_copy(b_hbm, b, in_sem.at[0])
    b_in.start()
    loads = []
    for i, half in enumerate((oc, c)):
        rows = pl.ds(pl.multiple_of(half * HALF, HALF), HALF)
        for j, (src, dst) in enumerate(((g_hbm, g), (e_hbm, e))):
            cp = pltpu.make_async_copy(src.at[0, rows], dst.at[rows], in_sem.at[1 + 2 * i + j])
            cp.start()
            loads.append(cp)

    barrier = pltpu.get_barrier_semaphore()

    def greet(to):
        pl.semaphore_signal(barrier, inc=1, device_id=to, device_id_type=MESH)

    greet(sib)
    near = ((2, 2), (2, 1), (2, 3), (1, 2), (3, 2), (1, 1), (1, 3), (3, 1), (3, 3), (2, 0), (0, 2), (1, 0), (3, 0), (0, 1), (0, 3))
    for dz in (4, 3, 5, 2, 6, 1, 7):
        greet(dev((t + dz) % NZ, x, y, c))
    for dx, dy in near:
        xx, yy = plane(dx, dy)
        greet(dev(t, xx, yy, c))
    for k in (2, 1, 3):
        greet(dev(t, (x + k) % NX, y, oc))
        greet(dev(t, x, (y + k) % NY, oc))

    b_in.wait()
    bs = jnp.concatenate(split3(b[...]), axis=0)

    def left(half, pair):
        rows = pl.ds(pl.multiple_of(half * HALF, HALF), HALF)
        pair[0].wait()
        acc = dot(bs, g[rows, :], NT)
        pair[1].wait()
        return fold(acc + dot(bs, e[rows, :], NT))

    own_part[...] = left(oc, loads[0:2])
    pl.semaphore_wait(barrier, 29)
    send(own_part, sib_part, core_s, core_r, sib)
    mine = left(c, loads[2:4])
    pos_one = jnp.where(c == 0, x, y)
    pos_two = jnp.where(c == 0, y, x)
    got(sib_part, core_r)
    one[pos_one] = mine + sib_part[...]
    for k in (2, 1, 3):
        to = dev(t, (x + k * oc) % NX, (y + k * c) % NY, c)
        send(one.at[pos_one], one.at[pos_one], one_s, one_r, to)
    got(one.at[pl.ds(0, 3)], one_r)
    slot = c * 4 + pos_two
    two[slot] = (one[0] + one[1]) + (one[2] + one[3])
    for k in (2, 1, 3):
        xx, yy = (x + k * c) % NX, (y + k * oc) % NY
        for cc in (c, oc):
            send(two.at[slot], two.at[slot], two_s, two_r, dev(t, xx, yy, cc))
    send(two.at[slot], two.at[slot], two_s, two_r, sib)
    got(two.at[pl.ds(0, 7)], two_r)
    for half in range(2):
        c_t[:, half * HALF : (half + 1) * HALF] = (two[4 * half] + two[4 * half + 1]) + (
            two[4 * half + 2] + two[4 * half + 3]
        )

    cs = jnp.concatenate(split3(c_t[...]), axis=0)
    for i, dx in enumerate((2, 1, 3, 0)):
        xx = (x + dx) % NX
        cols = pl.ds(pl.multiple_of(xx * 512, 512), 512)
        r = fold(dot(cs, g[:, cols]) + dot(cs, e[:, cols]))
        for yy in range(NY):
            for half in range(2):
                r_all[xx * NY + yy, half] = r[32 * half : 32 * half + 32, 128 * yy : 128 * yy + 128]
        four = pl.ds(xx * NY, NY)
        send(r_all.at[four, oc], r_sib.at[four], rc_s.at[i], rc_r.at[i], sib)

    gram = lax.dot_general(c_t[...], c_t[...], NT, precision=HIGH, preferred_element_type=f32)
    gbuf[t] = jnp.concatenate([gram[0:32], gram[32:64]], axis=1)
    for dz in (4, 3, 5, 2, 6, 1, 7):
        send(gbuf.at[t], gbuf.at[t], gr_s, gr_r, dev((t + dz) % NZ, x, y, c))

    for i, dx in enumerate((2, 1, 3, 0)):
        xx = (x + dx) % NX
        four = pl.ds(xx * NY, NY)
        got(r_sib.at[four], rc_r.at[i])
        for dy in (2, 1, 3, 0):
            yy = (y + dy) % NY
            n = xx * NY + yy
            summed = r_all[n, c] + r_sib[n]
            if dx == 0 and dy == 0:
                rbuf[n] = summed
            else:
                r_sib[n] = summed
                send(r_sib.at[n], rbuf.at[chip], xy_s, xy_r, dev(t, xx, yy, c))
    got(rbuf.at[pl.ds(0, 15)], xy_r)
    total = rbuf[0]
    for n in range(1, 16):
        total = total + rbuf[n]
    zbuf[t] = total
    for dz in (4, 3, 5, 2, 6, 1, 7):
        send(zbuf.at[t], zbuf.at[t], z_s, z_r, dev((t + dz) % NZ, x, y, c))

    got(gbuf.at[pl.ds(0, 7)], gr_r)
    packed = gbuf[0]
    for n in range(1, NZ):
        packed = packed + gbuf[n]
    rows = lax.broadcasted_iota(jnp.int32, (RANK, RANK), 0)
    lanes = lax.broadcasted_iota(jnp.int32, (RANK, RANK), 1)
    gram = jnp.concatenate([packed[:, 0:64], packed[:, 64:128]], axis=0)
    a = jnp.concatenate([gram, jnp.where(rows == lanes, 1.0, 0.0)], axis=1)
    aug[...] = eliminate(a, 0, 32)

    got(zbuf.at[pl.ds(0, 7)], z_r)
    total = zbuf[0]
    for n in range(1, NZ):
        total = total + zbuf[n]
    tb[chip, c] = total
    for dx, dy in near:
        xx, yy = plane(dx, dy)
        send(tb.at[chip, c], tb.at[chip, c], ag_s, ag_r, dev(t, xx, yy, c))

    inv = eliminate(aug[...], 32, 64)[:, RANK : 2 * RANK]
    o_t = lax.dot_general(inv, c_t[...], NN, precision=HIGH, preferred_element_type=f32)
    ortho = o_t.T
    o_hi, o_lo = split2(ortho)
    op_ref[0:HID, :] = jnp.concatenate([o_hi, o_hi, o_lo], axis=1)
    op_ref[HID : HID + 16, :] = op_ref[pl.ds(pl.multiple_of(d * 16, 16), 16), :]
    i_hi, i_lo = split2(inv * (1.0 / 32.0))
    inv_parts = jnp.concatenate([i_hi, i_hi, i_lo], axis=1)

    got(tb.at[pl.ds(0, 15), 0], ag_r)
    send(tb.at[:, c], tb.at[:, c], fw_s, fw_r, sib)
    got(tb.at[:, oc], fw_r)
    for n in range(0, 16, 2):
        blk = jnp.concatenate(
            [jnp.concatenate([tb[m, 0], tb[m, 1]], axis=0) for m in (n, n + 1)], axis=1
        )
        t_hi, t_lo = split2(blk)
        bn_ref[:, 128 * n : 128 * n + 256] = dot(inv_parts, jnp.concatenate([t_hi, t_lo, t_hi], axis=0))

    sent(own_part, core_s)
    sent(one.at[pl.ds(0, 3)], one_s)
    sent(two.at[pl.ds(0, 7)], two_s)
    for i in range(4):
        sent(r_sib.at[pl.ds(0, NY)], rc_s.at[i])
    sent(rbuf.at[pl.ds(0, 15)], xy_s)
    sent(zbuf.at[pl.ds(0, 7)], z_s)
    sent(gbuf.at[pl.ds(0, 7)], gr_s)
    sent(rbuf.at[pl.ds(0, 15)], ag_s)
    sent(rbuf, fw_s)


def exchange(g, e, b_t):
    any_ = pl.BlockSpec(memory_space=pl.ANY)
    vm = pl.BlockSpec(memory_space=VMEM)
    dma = pltpu.SemaphoreType.DMA
    return pl.pallas_call(
        exchange_kernel,
        name="exchange",
        out_shape=(
            jax.ShapeDtypeStruct((RANK, D), f32),
            jax.ShapeDtypeStruct((HID + 16, 3 * RANK), bf16),
        ),
        in_specs=[any_] * 3,
        out_specs=(vm, vm),
        scratch_shapes=[
            VMEM((HID, D), bf16),
            VMEM((HID, D), bf16),
            VMEM((RANK, D), f32),
            VMEM((RANK, HALF), f32),
            VMEM((RANK, HALF), f32),
            VMEM((4, RANK, HALF), f32),
            VMEM((8, RANK, HALF), f32),
            VMEM((RANK, HID), f32),
            VMEM((16, 2, 32, 128), f32),
            VMEM((16, 32, 128), f32),
            VMEM((16, 32, 128), f32),
            VMEM((NZ, 32, 128), f32),
            VMEM((32, 128), f32),
            VMEM((NZ, 32, 128), f32),
            VMEM((16, 2, 32, 128), f32),
            VMEM((RANK, 2 * RANK), f32),
            dma((5,)),
            dma, dma, dma, dma, dma, dma,
            dma((4,)), dma((4,)),
            dma, dma, dma, dma, dma, dma, dma, dma, dma, dma,
        ],
        compiler_params=pltpu.CompilerParams(
            collective_id=0, has_side_effects=True, vmem_limit_bytes=24 << 20
        ),
    )(g, e, b_t)


def apply_kernel(
    bn_ref, op_ref, g_ref, e_ref, w_ref, m_ref, s_ref, ne_hbm, bo_ref, wo_ref, mo_ref, so_ref, ne, sem
):
    op = op_ref[...]
    copies = []
    for j in range(8):
        cols = slice(256 * j, 256 * j + 256)
        bn = bn_ref[:, cols]
        bo_ref[:, cols] = bn
        hi, lo = split2(bn)
        approx = dot(op, jnp.concatenate([hi, lo, hi], axis=0))
        merged = g_ref[0, :, cols].astype(f32) + e_ref[0, :, cols].astype(f32)
        ne[:, cols] = (merged - approx[0:HID]).astype(bf16)
        cp = pltpu.make_async_copy(ne.at[:, cols], ne_hbm.at[0, :, cols], sem.at[j])
        cp.start()
        copies.append(cp)
        update = approx[HID : HID + 16]
        moment_next = beta_first * m_ref[:, cols] + (1.0 - beta_first) * update
        second_next = beta_second * s_ref[:, cols] + (1.0 - beta_second) * update * update
        mo_ref[:, cols] = moment_next
        so_ref[:, cols] = second_next
        wo_ref[:, cols] = w_ref[:, cols] - step_size * (moment_next / corr_first) / (
            jnp.sqrt(second_next / corr_second) + adam_eps
        )
    for cp in copies:
        cp.wait()


def apply(bn, op, g, e, w, m, s):
    vm = pl.BlockSpec(memory_space=VMEM)
    rows = jax.ShapeDtypeStruct(w.shape, f32)
    return pl.pallas_call(
        apply_kernel,
        name="apply",
        out_shape=(
            jax.ShapeDtypeStruct(g.shape, bf16),
            jax.ShapeDtypeStruct((RANK, D), f32),
            rows, rows, rows,
        ),
        in_specs=[vm] * 7,
        out_specs=(pl.BlockSpec(memory_space=pl.ANY), vm, vm, vm, vm),
        scratch_shapes=[VMEM((HID, D), bf16), pltpu.SemaphoreType.DMA((8,))],
        compiler_params=pltpu.CompilerParams(vmem_limit_bytes=24 << 20),
    )(bn, op, g, e, w, m, s)


def body(grads, errors, basis, weight, moment, second):
    bn, op = exchange(grads, errors, basis.T)
    new_errors, bo, w, m, s = apply(bn, op, grads, errors, weight, moment, second)
    return new_errors, bo.T, w, m, s


def solution(mesh):
    placed = (
        P("dp", "tensor", None),
        P("dp", "tensor", None),
        P(),
        P(("tensor", "dp"), None),
        P(("tensor", "dp"), None),
        P(("tensor", "dp"), None),
    )
    return jax.shard_map(
        body,
        mesh=mesh,
        in_specs=placed,
        out_specs=(
            P("dp", "tensor", None),
            P(),
            P(("tensor", "dp"), None),
            P(("tensor", "dp"), None),
            P(("tensor", "dp"), None),
        ),
        check_vma=False,
    )
```

```python
import jax
import jax.numpy as jnp
from jax import lax
from jax.experimental import pallas as pl
from jax.experimental.pallas import tpu as pltpu
from jax.sharding import PartitionSpec as P

beta_first = 0.9
beta_second = 0.95
step_size = 0.1
adam_eps = 1e-08
corr_first = 1.0 - 0.9**10
corr_second = 1.0 - 0.95**10

MESH = pl.DeviceIdType.MESH
VMEM = pltpu.VMEM
f32, bf16 = jnp.float32, jnp.bfloat16
D, RANK, HID, HALF = 2048, 64, 512, 256
NX, NY, NZ = 4, 4, 8
NN = (((1,), (0,)), ((), ()))
NT = (((1,), (1,)), ((), ()))
TN = (((0,), (0,)), ((), ()))
HIGH = lax.Precision.HIGHEST


def split3(v):
    hi = v.astype(bf16)
    rest = v - hi.astype(f32)
    mid = rest.astype(bf16)
    lo = (rest - mid.astype(f32)).astype(bf16)
    return hi, mid, lo


def split2(v):
    hi = v.astype(bf16)
    return hi, (v - hi.astype(f32)).astype(bf16)


def dot(a, b, dims=NN):
    return lax.dot_general(a, b, dims, preferred_element_type=f32)


def fold(v):
    return v[0:RANK] + v[RANK : 2 * RANK] + v[2 * RANK : 3 * RANK]


def sub_row(v, k):
    return jnp.broadcast_to(v[k : k + 1, :], v.shape)


def inverse_factor(a):
    blocks = [a[8 * v : 8 * v + 8] for v in range(8)]
    sub = lax.broadcasted_iota(jnp.int32, (8, 2 * RANK), 0)
    lane = lax.broadcasted_iota(jnp.int32, (8, 2 * RANK), 1)
    for v in range(8):
        cols = {
            u: [jnp.broadcast_to(blocks[u][:, 8 * v + j : 8 * v + j + 1], (8, 2 * RANK)) for j in range(8)]
            for u in range(v, 8)
        }
        for k in range(8):
            over = 1.0 / sub_row(cols[v][k], k)
            later = [sub_row(cols[v][j], k) for j in range(k + 1, 8)]
            row = sub_row(blocks[v], k)
            for u in range(v, 8):
                times = cols[u][k] * over
                if u == v:
                    times = jnp.where(sub > k, times, 0.0)
                for j in range(k + 1, 8):
                    cols[u][j] = cols[u][j] - times * later[j - k - 1]
                blocks[u] = blocks[u] - times * row
    out = []
    for v in range(8):
        pivots = jnp.sum(jnp.where(lane == sub + 8 * v, blocks[v], 0.0), axis=1, keepdims=True)
        out.append(blocks[v] / lax.sqrt(pivots))
    return jnp.concatenate(out, axis=0)[:, RANK:]


FAR = ((2, 2), (2, 1), (2, 3), (1, 2), (3, 2), (1, 1), (1, 3), (3, 1), (3, 3), (2, 0), (0, 2), (1, 0), (3, 0), (0, 1), (0, 3))
ZFAR = (4, 3, 5, 2, 6, 1, 7)


def exchange_kernel(
    g_hbm, e_hbm, b_hbm, tb, op_ref, ip_ref, g, e,
    b, p_send, p_recv, c_buf, c_t, r_all, r_sib, rbuf, zbuf, gbuf,
    in_sem, p_s, p_r, c_s, c_r, rc_s, rc_r, xy_s, xy_r, z_s, z_r, gr_s, gr_r, ag_s, ag_r, fw_s, fw_r,
):
    t = lax.axis_index("tensor")
    d = lax.axis_index("dp")
    x, y, c = d // 8, (d // 2) % NY, d % 2
    oc = 1 - c
    chip = x * NY + y

    def dev(tt, xx, yy, cc):
        return (tt, (xx * NY + yy) * 2 + cc)

    sib = dev(t, x, y, oc)

    def send(src, dst, ss, rs, to):
        pltpu.make_async_remote_copy(
            src_ref=src, dst_ref=dst, send_sem=ss, recv_sem=rs, device_id=to, device_id_type=MESH
        ).start()

    def got(ref, rs):
        pltpu.make_async_remote_copy(
            src_ref=ref, dst_ref=ref, send_sem=p_s, recv_sem=rs, device_id=sib, device_id_type=MESH
        ).wait_recv()

    def sent(ref, ss):
        pltpu.make_async_remote_copy(
            src_ref=ref, dst_ref=ref, send_sem=ss, recv_sem=p_r, device_id=sib, device_id_type=MESH
        ).wait_send()

    barrier = pltpu.get_barrier_semaphore()

    def greet(to):
        pl.semaphore_signal(barrier, inc=1, device_id=to, device_id_type=MESH)

    b_in = pltpu.make_async_copy(b_hbm, b, in_sem.at[0])
    b_in.start()
    x_far = (x + 2) % NX
    x_near = x + 1 - 2 * (x % 2)
    x_mid = x_far + 1 - 2 * (x_far % 2)
    halves = (x_far // 2, x // 2)
    loads = []
    for i, half in enumerate(halves):
        for j, (src, dst) in enumerate(((g_hbm, g), (e_hbm, e))):
            for k in range(2):
                rows = pl.ds(pl.multiple_of(half * HALF + 128 * k, 128), 128)
                cp = pltpu.make_async_copy(src.at[0, rows], dst.at[rows], in_sem.at[1 + 4 * i + 2 * j + k])
                cp.start()
                loads.append(cp)
        if i == 0:
            for dz in ZFAR:
                greet(dev((t + dz) % NZ, x, y, c))
            for dx, dy in FAR:
                for cc in (c, oc):
                    greet(dev(t, (x + dx) % NX, (y + dy) % NY, cc))
            greet(sib)

    b_in.wait()
    bs = jnp.concatenate(split3(b[...]), axis=0)
    for i, half in enumerate(halves):
        rows = pl.ds(pl.multiple_of(half * HALF, HALF), HALF)
        loads[4 * i].wait()
        loads[4 * i + 1].wait()
        acc = dot(bs, g[rows, :], NT)
        loads[4 * i + 2].wait()
        loads[4 * i + 3].wait()
        part = fold(acc + dot(bs, e[rows, :], NT))
        for j in range(2):
            for k in range(8):
                p_send[16 * half + 8 * j + k] = part[8 * k : 8 * k + 8, 128 * j : 128 * j + 128]
        if i == 0:
            pl.semaphore_wait(barrier, 38)
        for xx in ((x_far, x_mid), (x_near, x))[i]:
            for dy in (2, 1, 3, 0):
                yy = (y + dy) % NY
                for cc in (oc, c):
                    n = (xx * NY + yy) * 2 + cc
                    if xx is x and dy == 0 and cc is c:
                        p_recv[n] = p_send[n]
                    else:
                        send(p_send.at[n], p_recv.at[d], p_s, p_r, dev(t, xx, yy, cc))
    got(p_recv.at[pl.ds(0, 31)], p_r)
    total = p_recv[0]
    for n in range(1, 32):
        total = total + p_recv[n]
    c_buf[d] = total
    for dx, dy in FAR + ((0, 0),):
        for cc in (oc, c):
            if not (dx == 0 and dy == 0 and cc is c):
                send(c_buf.at[d], c_buf.at[d], c_s, c_r, dev(t, (x + dx) % NX, (y + dy) % NY, cc))
    got(c_buf.at[pl.ds(0, 31)], c_r)
    for j in range(4):
        c_t[:, 128 * j : 128 * j + 128] = c_buf[8 * j : 8 * j + 8].reshape(RANK, 128)

    cs = jnp.concatenate(split3(c_t[...]), axis=0)

    def right(i, dx):
        xx = (x + dx) % NX
        cols = pl.ds(pl.multiple_of(xx * 512, 512), 512)
        r = fold(dot(cs, g[:, cols]) + dot(cs, e[:, cols]))
        for yy in range(NY):
            for half in range(2):
                r_all[xx * NY + yy, half] = r[32 * half : 32 * half + 32, 128 * yy : 128 * yy + 128]
        four = pl.ds(xx * NY, NY)
        send(r_all.at[four, oc], r_sib.at[four], rc_s.at[i], rc_r.at[i], sib)

    def scatter(i, dx):
        xx = (x + dx) % NX
        four = pl.ds(xx * NY, NY)
        got(r_sib.at[four], rc_r.at[i])
        if dx:
            r_sib[four] = r_all[four, c] + r_sib[four]
        else:
            for dy in (2, 1, 3, 0):
                n = xx * NY + (y + dy) % NY
                summed = r_all[n, c] + r_sib[n]
                if dy:
                    r_sib[n] = summed
                else:
                    rbuf[n] = summed
        for dy in (2, 1, 3, 0):
            yy = (y + dy) % NY
            if dx or dy:
                send(r_sib.at[xx * NY + yy], rbuf.at[chip], xy_s, xy_r, dev(t, xx, yy, c))

    right(0, 2)
    right(1, 1)
    right(2, 3)
    scatter(0, 2)
    right(3, 0)
    scatter(1, 1)
    scatter(2, 3)
    scatter(3, 0)
    gram = lax.dot_general(c_t[...], c_t[...], NT, precision=HIGH, preferred_element_type=f32)
    gbuf[t] = jnp.concatenate([gram[0:32], gram[32:64]], axis=1)
    for dz in ZFAR:
        send(gbuf.at[t], gbuf.at[t], gr_s, gr_r, dev((t + dz) % NZ, x, y, c))

    got(rbuf.at[pl.ds(0, 15)], xy_r)
    total = rbuf[0]
    for n in range(1, 16):
        total = total + rbuf[n]
    zbuf[t] = total
    for dz in ZFAR:
        send(zbuf.at[t], zbuf.at[t], z_s, z_r, dev((t + dz) % NZ, x, y, c))

    got(gbuf.at[pl.ds(0, 7)], gr_r)
    packed = gbuf[0]
    for n in range(1, NZ):
        packed = packed + gbuf[n]
    rows = lax.broadcasted_iota(jnp.int32, (RANK, RANK), 0)
    lanes = lax.broadcasted_iota(jnp.int32, (RANK, RANK), 1)
    gram = jnp.concatenate([packed[:, 0:64], packed[:, 64:128]], axis=0)
    a = jnp.concatenate([gram, jnp.where(rows == lanes, 1.0, 0.0)], axis=1)
    inv = inverse_factor(a)
    o_t = lax.dot_general(inv, c_t[...], NN, precision=HIGH, preferred_element_type=f32)
    o_hi, o_lo = split2(o_t.T)
    op_ref[0:HID, :] = jnp.concatenate([o_hi, o_hi, o_lo], axis=1)
    op_ref[HID : HID + 16, :] = op_ref[pl.ds(pl.multiple_of(d * 16, 16), 16), :]
    i_hi, i_lo = split2(inv * (1.0 / 32.0))
    ip_ref[...] = jnp.concatenate([i_hi, i_hi, i_lo], axis=1)

    got(zbuf.at[pl.ds(0, 7)], z_r)
    total = zbuf[0]
    for n in range(1, NZ):
        total = total + zbuf[n]
    tb[chip, c] = total
    for dx, dy in FAR:
        send(tb.at[chip, c], tb.at[chip, c], ag_s, ag_r.at[chip], dev(t, (x + dx) % NX, (y + dy) % NY, c))
    send(tb.at[chip, c], tb.at[chip, c], fw_s, fw_r.at[chip], sib)

    for dx, dy in FAR:
        n = ((x + dx) % NX) * NY + (y + dy) % NY
        got(tb.at[n, c], ag_r.at[n])
        send(tb.at[n, c], tb.at[n, c], fw_s, fw_r.at[n], sib)
    for dx, dy in ((0, 0),) + FAR:
        n = ((x + dx) % NX) * NY + (y + dy) % NY
        got(tb.at[n, oc], fw_r.at[n])

    sent(p_recv.at[pl.ds(0, 31)], p_s)
    sent(p_recv.at[pl.ds(0, 31)], c_s)
    for i in range(4):
        sent(r_sib.at[pl.ds(0, NY)], rc_s.at[i])
    sent(rbuf.at[pl.ds(0, 15)], xy_s)
    sent(zbuf.at[pl.ds(0, 7)], z_s)
    sent(gbuf.at[pl.ds(0, 7)], gr_s)
    sent(rbuf.at[pl.ds(0, 15)], ag_s)
    sent(rbuf, fw_s)


def exchange(g, e, b_t):
    hbm = pl.BlockSpec(memory_space=pltpu.HBM)
    vm = pl.BlockSpec(memory_space=VMEM)
    dma = pltpu.SemaphoreType.DMA
    return pl.pallas_call(
        exchange_kernel,
        name="exchange",
        out_shape=(
            jax.ShapeDtypeStruct((16, 2, 32, 128), f32),
            jax.ShapeDtypeStruct((HID + 16, 3 * RANK), bf16),
            jax.ShapeDtypeStruct((RANK, 3 * RANK), bf16),
            jax.ShapeDtypeStruct((HID, D), bf16),
            jax.ShapeDtypeStruct((HID, D), bf16),
        ),
        in_specs=[hbm] * 3,
        out_specs=(vm,) * 5,
        scratch_shapes=[
            VMEM((RANK, D), f32),
            VMEM((32, 8, 128), f32),
            VMEM((32, 8, 128), f32),
            VMEM((32, 8, 128), f32),
            VMEM((RANK, HID), f32),
            VMEM((16, 2, 32, 128), f32),
            VMEM((16, 32, 128), f32),
            VMEM((16, 32, 128), f32),
            VMEM((NZ, 32, 128), f32),
            VMEM((NZ, 32, 128), f32),
            dma((9,)),
            dma, dma, dma, dma,
            dma((4,)), dma((4,)),
            dma, dma, dma, dma, dma, dma,
            dma, dma((16,)), dma, dma((16,)),
        ],
        compiler_params=pltpu.CompilerParams(
            collective_id=0, has_side_effects=True, vmem_limit_bytes=24 << 20
        ),
    )(*(pltpu.with_memory_space_constraint(v, pltpu.HBM) for v in (g, e, b_t)))


def apply_kernel(
    tb_ref, op_ref, ip_ref, g_ref, e_ref, w_ref, m_ref, s_ref, ne_hbm, bo_hbm, wo_hbm, mo_hbm, so_hbm,
    bn, ne, wo, mo, so, sem,
):
    op, ip = op_ref[...], ip_ref[...]
    copies = []

    def out(src, dst):
        cp = pltpu.make_async_copy(src, dst, sem.at[len(copies)])
        cp.start()
        copies.append(cp)

    for j in range(8):
        cols = slice(256 * j, 256 * j + 256)
        block = jnp.concatenate([tb_ref[n].reshape(RANK, 128) for n in (2 * j, 2 * j + 1)], axis=1)
        hi, lo = split2(block)
        right = dot(ip, jnp.concatenate([hi, lo, hi], axis=0))
        bn[:, cols] = right
        hi, lo = split2(right)
        approx = dot(op, jnp.concatenate([hi, lo, hi], axis=0))
        merged = g_ref[:, cols].astype(f32) + e_ref[:, cols].astype(f32)
        ne[:, cols] = (merged - approx[0:HID]).astype(bf16)
        out(ne.at[:, cols], ne_hbm.at[0, :, cols])
        update = approx[HID : HID + 16]
        moment_next = beta_first * m_ref[:, cols] + (1.0 - beta_first) * update
        second_next = beta_second * s_ref[:, cols] + (1.0 - beta_second) * update * update
        mo[:, cols] = moment_next
        so[:, cols] = second_next
        wo[:, cols] = w_ref[:, cols] - step_size * (moment_next / corr_first) / (
            jnp.sqrt(second_next / corr_second) + adam_eps
        )
    out(bn, bo_hbm)
    out(mo, mo_hbm)
    out(so, so_hbm)
    out(wo, wo_hbm)
    for cp in copies:
        cp.wait()


def apply(tb, op, ip, g, e, w, m, s):
    vm = pl.BlockSpec(memory_space=VMEM)
    rows = jax.ShapeDtypeStruct(w.shape, f32)
    return pl.pallas_call(
        apply_kernel,
        name="apply",
        out_shape=(
            jax.ShapeDtypeStruct((1, HID, D), bf16),
            jax.ShapeDtypeStruct((RANK, D), f32),
            rows, rows, rows,
        ),
        in_specs=[vm] * 8,
        out_specs=(pl.BlockSpec(memory_space=pltpu.HBM),) * 5,
        scratch_shapes=[VMEM((RANK, D), f32), VMEM((HID, D), bf16)] + [VMEM(w.shape, f32)] * 3 + [pltpu.SemaphoreType.DMA((12,))],
        compiler_params=pltpu.CompilerParams(vmem_limit_bytes=24 << 20),
    )(tb, op, ip, g, e, w, m, s)


def body(grads, errors, basis, weight, moment, second):
    tb, op, ip, g, e = exchange(grads, errors, basis.T)
    new_errors, bo, w, m, s = apply(tb, op, ip, g, e, weight, moment, second)
    return new_errors, bo.T, w, m, s


def solution(mesh):
    placed = (
        P("dp", "tensor", None),
        P("dp", "tensor", None),
        P(),
        P(("tensor", "dp"), None),
        P(("tensor", "dp"), None),
        P(("tensor", "dp"), None),
    )
    return jax.shard_map(
        body,
        mesh=mesh,
        in_specs=placed,
        out_specs=(
            P("dp", "tensor", None),
            P(),
            P(("tensor", "dp"), None),
            P(("tensor", "dp"), None),
            P(("tensor", "dp"), None),
        ),
        check_vma=False,
    )
```

```python
import jax
import jax.numpy as jnp
from jax import lax
from jax.experimental import pallas as pl
from jax.experimental.pallas import tpu as pltpu
from jax.sharding import PartitionSpec as P

beta_first = 0.9
beta_second = 0.95
step_size = 0.1
adam_eps = 1e-08
corr_first = 1.0 - 0.9**10
corr_second = 1.0 - 0.95**10

MESH = pl.DeviceIdType.MESH
VMEM = pltpu.VMEM
f32, bf16 = jnp.float32, jnp.bfloat16
D, RANK, HID, HALF, WIDE = 2048, 64, 512, 256, 1024
NX, NY, NZ = 4, 4, 8
NN = (((1,), (0,)), ((), ()))
NT = (((1,), (1,)), ((), ()))
TN = (((0,), (0,)), ((), ()))
HIGH = lax.Precision.HIGHEST


def split3(v):
    hi = v.astype(bf16)
    rest = v - hi.astype(f32)
    mid = rest.astype(bf16)
    lo = (rest - mid.astype(f32)).astype(bf16)
    return hi, mid, lo


def split2(v):
    hi = v.astype(bf16)
    return hi, (v - hi.astype(f32)).astype(bf16)


def dot(a, b, dims=NN):
    return lax.dot_general(a, b, dims, preferred_element_type=f32)


def fold(v):
    return v[0:RANK] + v[RANK : 2 * RANK] + v[2 * RANK : 3 * RANK]


def sub_row(v, k):
    return jnp.broadcast_to(v[k : k + 1, :], v.shape)


def inverse_factor(a):
    blocks = [a[8 * v : 8 * v + 8] for v in range(8)]
    sub = lax.broadcasted_iota(jnp.int32, (8, 2 * RANK), 0)
    lane = lax.broadcasted_iota(jnp.int32, (8, 2 * RANK), 1)
    for v in range(8):
        cols = {
            u: [jnp.broadcast_to(blocks[u][:, 8 * v + j : 8 * v + j + 1], (8, 2 * RANK)) for j in range(8)]
            for u in range(v, 8)
        }
        for k in range(8):
            over = 1.0 / sub_row(cols[v][k], k)
            later = [sub_row(cols[v][j], k) for j in range(k + 1, 8)]
            row = sub_row(blocks[v], k)
            for u in range(v, 8):
                times = cols[u][k] * over
                if u == v:
                    times = jnp.where(sub > k, times, 0.0)
                for j in range(k + 1, 8):
                    cols[u][j] = cols[u][j] - times * later[j - k - 1]
                blocks[u] = blocks[u] - times * row
    out = []
    for v in range(8):
        pivots = jnp.sum(jnp.where(lane == sub + 8 * v, blocks[v], 0.0), axis=1, keepdims=True)
        out.append(blocks[v] / lax.sqrt(pivots))
    return jnp.concatenate(out, axis=0)[:, RANK:]


FAR = ((2, 2), (2, 1), (2, 3), (1, 2), (3, 2), (1, 1), (1, 3), (3, 1), (3, 3), (2, 0), (0, 2), (1, 0), (3, 0), (0, 1), (0, 3))
ZFAR = (4, 3, 5, 2, 6, 1, 7)


def exchange_kernel(
    g_hbm, e_hbm, b_hbm, tb, op_ref, ip_ref, g, e,
    b, p_send, p_recv, c_buf, c_t, m_send, m_recv, s_hi, s_lo, r_all, rbuf, zbuf, gbuf,
    in_sem, p_s, p_r, c_s, c_r, ms_s, ms_r, xy_s, xy_r, z_s, z_r, gr_s, gr_r, ag_s, ag_r, fw_s, fw_r,
):
    t = lax.axis_index("tensor")
    d = lax.axis_index("dp")
    x, y, c = d // 8, (d // 2) % NY, d % 2
    oc = 1 - c
    chip = x * NY + y

    def dev(tt, xx, yy, cc):
        return (tt, (xx * NY + yy) * 2 + cc)

    sib = dev(t, x, y, oc)

    def send(src, dst, ss, rs, to):
        pltpu.make_async_remote_copy(
            src_ref=src, dst_ref=dst, send_sem=ss, recv_sem=rs, device_id=to, device_id_type=MESH
        ).start()

    def got(ref, rs):
        pltpu.make_async_remote_copy(
            src_ref=ref, dst_ref=ref, send_sem=p_s, recv_sem=rs, device_id=sib, device_id_type=MESH
        ).wait_recv()

    def sent(ref, ss):
        pltpu.make_async_remote_copy(
            src_ref=ref, dst_ref=ref, send_sem=ss, recv_sem=p_r, device_id=sib, device_id_type=MESH
        ).wait_send()

    barrier = pltpu.get_barrier_semaphore()

    def greet(to):
        pl.semaphore_signal(barrier, inc=1, device_id=to, device_id_type=MESH)

    b_in = pltpu.make_async_copy(b_hbm, b, in_sem.at[0])
    b_in.start()
    x_far = (x + 2) % NX
    x_near = x + 1 - 2 * (x % 2)
    x_mid = x_far + 1 - 2 * (x_far % 2)
    halves = (x_far // 2, x // 2)
    loads = []
    for i, half in enumerate(halves):
        for j, (src, dst) in enumerate(((g_hbm, g), (e_hbm, e))):
            for k in range(2):
                rows = pl.ds(pl.multiple_of(half * HALF + 128 * k, 128), 128)
                cp = pltpu.make_async_copy(src.at[0, rows], dst.at[rows], in_sem.at[1 + 4 * i + 2 * j + k])
                cp.start()
                loads.append(cp)
        if i == 0:
            for dz in ZFAR:
                greet(dev((t + dz) % NZ, x, y, c))
            for dx, dy in FAR:
                for cc in (c, oc):
                    greet(dev(t, (x + dx) % NX, (y + dy) % NY, cc))
            greet(sib)

    b_in.wait()
    bs = jnp.concatenate(split3(b[...]), axis=0)
    for i, half in enumerate(halves):
        rows = pl.ds(pl.multiple_of(half * HALF, HALF), HALF)
        loads[4 * i].wait()
        loads[4 * i + 1].wait()
        acc = dot(bs, g[rows, :], NT)
        loads[4 * i + 2].wait()
        loads[4 * i + 3].wait()
        part = fold(acc + dot(bs, e[rows, :], NT))
        for j in range(2):
            for k in range(8):
                p_send[16 * half + 8 * j + k] = part[8 * k : 8 * k + 8, 128 * j : 128 * j + 128]
        if i == 0:
            pl.semaphore_wait(barrier, 38)
        for xx in ((x_far, x_mid), (x_near, x))[i]:
            for dy in (2, 1, 3, 0):
                yy = (y + dy) % NY
                for cc in (oc, c):
                    n = (xx * NY + yy) * 2 + cc
                    if xx is x and dy == 0 and cc is c:
                        p_recv[n] = p_send[n]
                    else:
                        send(p_send.at[n], p_recv.at[d], p_s, p_r, dev(t, xx, yy, cc))
    theirs = pl.ds(pl.multiple_of(oc * WIDE, WIDE), WIDE)
    ours = pl.ds(pl.multiple_of(c * WIDE, WIDE), WIDE)
    for k in range(4):
        rows = pl.ds(128 * k, 128)
        m_send[rows, :] = g[rows, theirs].astype(f32) + e[rows, theirs].astype(f32)
        send(m_send.at[rows], m_recv.at[rows], ms_s.at[k], ms_r.at[k], sib)
    got(p_recv.at[pl.ds(0, 31)], p_r)
    total = p_recv[0]
    for n in range(1, 32):
        total = total + p_recv[n]
    c_buf[d] = total
    for dx, dy in FAR + ((0, 0),):
        for cc in (oc, c):
            if not (dx == 0 and dy == 0 and cc is c):
                send(c_buf.at[d], c_buf.at[d], c_s, c_r, dev(t, (x + dx) % NX, (y + dy) % NY, cc))
    for k in range(4):
        rows = pl.ds(128 * k, 128)
        got(m_recv.at[rows], ms_r.at[k])
        pair = (g[rows, ours].astype(f32) + e[rows, ours].astype(f32)) + m_recv[rows, :]
        s_hi[rows, :], s_lo[rows, :] = split2(pair)
    got(c_buf.at[pl.ds(0, 31)], c_r)
    for j in range(4):
        c_t[:, 128 * j : 128 * j + 128] = c_buf[8 * j : 8 * j + 8].reshape(RANK, 128)

    cs = jnp.concatenate(split3(c_t[...]), axis=0)

    for dx in (2, 0, 1, 3):
        xx = (x + dx) % NX
        cols = pl.ds(pl.multiple_of(xx * 256, 256), 256)
        r = fold(dot(cs, s_hi[:, cols]) + dot(cs, s_lo[:, cols]))
        for yy in range(NY):
            half, blk = yy % 2, yy // 2
            r_all[xx * NY + yy] = r[32 * half : 32 * half + 32, 128 * blk : 128 * blk + 128]
        for dy in (2, 1, 3, 0):
            yy = (y + dy) % NY
            n = xx * NY + yy
            if dx or dy:
                send(r_all.at[n], rbuf.at[chip], xy_s, xy_r, dev(t, xx, yy, c))
            else:
                rbuf[chip] = r_all[chip]
    gram = lax.dot_general(c_t[...], c_t[...], NT, precision=HIGH, preferred_element_type=f32)
    gbuf[t] = jnp.concatenate([gram[0:32], gram[32:64]], axis=1)
    for dz in ZFAR:
        send(gbuf.at[t], gbuf.at[t], gr_s, gr_r, dev((t + dz) % NZ, x, y, c))

    got(rbuf.at[pl.ds(0, 15)], xy_r)
    total = rbuf[0]
    for n in range(1, 16):
        total = total + rbuf[n]
    zbuf[t] = total
    for dz in ZFAR:
        send(zbuf.at[t], zbuf.at[t], z_s, z_r, dev((t + dz) % NZ, x, y, c))

    got(gbuf.at[pl.ds(0, 7)], gr_r)
    packed = gbuf[0]
    for n in range(1, NZ):
        packed = packed + gbuf[n]
    rows = lax.broadcasted_iota(jnp.int32, (RANK, RANK), 0)
    lanes = lax.broadcasted_iota(jnp.int32, (RANK, RANK), 1)
    gram = jnp.concatenate([packed[:, 0:64], packed[:, 64:128]], axis=0)
    a = jnp.concatenate([gram, jnp.where(rows == lanes, 1.0, 0.0)], axis=1)
    inv = inverse_factor(a)
    o_t = lax.dot_general(inv, c_t[...], NN, precision=HIGH, preferred_element_type=f32)
    o_hi, o_lo = split2(o_t.T)
    op_ref[0:HID, :] = jnp.concatenate([o_hi, o_hi, o_lo], axis=1)
    op_ref[HID : HID + 16, :] = op_ref[pl.ds(pl.multiple_of(d * 16, 16), 16), :]
    i_hi, i_lo = split2(inv * (1.0 / 32.0))
    ip_ref[...] = jnp.concatenate([i_hi, i_hi, i_lo], axis=1)

    got(zbuf.at[pl.ds(0, 7)], z_r)
    total = zbuf[0]
    for n in range(1, NZ):
        total = total + zbuf[n]
    tb[chip, c] = total
    for dx, dy in FAR:
        send(tb.at[chip, c], tb.at[chip, c], ag_s, ag_r.at[chip], dev(t, (x + dx) % NX, (y + dy) % NY, c))
    send(tb.at[chip, c], tb.at[chip, c], fw_s, fw_r.at[chip], sib)

    for dx, dy in FAR:
        n = ((x + dx) % NX) * NY + (y + dy) % NY
        got(tb.at[n, c], ag_r.at[n])
        send(tb.at[n, c], tb.at[n, c], fw_s, fw_r.at[n], sib)
    for dx, dy in ((0, 0),) + FAR:
        n = ((x + dx) % NX) * NY + (y + dy) % NY
        got(tb.at[n, oc], fw_r.at[n])

    sent(p_recv.at[pl.ds(0, 31)], p_s)
    sent(p_recv.at[pl.ds(0, 31)], c_s)
    for k in range(4):
        sent(m_recv.at[pl.ds(128 * k, 128)], ms_s.at[k])
    sent(rbuf.at[pl.ds(0, 15)], xy_s)
    sent(zbuf.at[pl.ds(0, 7)], z_s)
    sent(gbuf.at[pl.ds(0, 7)], gr_s)
    sent(rbuf.at[pl.ds(0, 15)], ag_s)
    sent(rbuf, fw_s)


def exchange(g, e, b_t):
    hbm = pl.BlockSpec(memory_space=pltpu.HBM)
    vm = pl.BlockSpec(memory_space=VMEM)
    dma = pltpu.SemaphoreType.DMA
    return pl.pallas_call(
        exchange_kernel,
        name="exchange",
        out_shape=(
            jax.ShapeDtypeStruct((16, 2, 32, 128), f32),
            jax.ShapeDtypeStruct((HID + 16, 3 * RANK), bf16),
            jax.ShapeDtypeStruct((RANK, 3 * RANK), bf16),
            jax.ShapeDtypeStruct((HID, D), bf16),
            jax.ShapeDtypeStruct((HID, D), bf16),
        ),
        in_specs=[hbm] * 3,
        out_specs=(vm,) * 5,
        scratch_shapes=[
            VMEM((RANK, D), f32),
            VMEM((32, 8, 128), f32),
            VMEM((32, 8, 128), f32),
            VMEM((32, 8, 128), f32),
            VMEM((RANK, HID), f32),
            VMEM((HID, WIDE), f32),
            VMEM((HID, WIDE), f32),
            VMEM((HID, WIDE), bf16),
            VMEM((HID, WIDE), bf16),
            VMEM((16, 32, 128), f32),
            VMEM((16, 32, 128), f32),
            VMEM((NZ, 32, 128), f32),
            VMEM((NZ, 32, 128), f32),
            dma((9,)),
            dma, dma, dma, dma,
            dma((4,)), dma((4,)),
            dma, dma, dma, dma, dma, dma,
            dma, dma((16,)), dma, dma((16,)),
        ],
        compiler_params=pltpu.CompilerParams(
            collective_id=0, has_side_effects=True, vmem_limit_bytes=24 << 20
        ),
    )(*(pltpu.with_memory_space_constraint(v, pltpu.HBM) for v in (g, e, b_t)))


def apply_kernel(
    tb_ref, op_ref, ip_ref, g_ref, e_ref, w_ref, m_ref, s_ref, ne_hbm, bo_hbm, wo_hbm, mo_hbm, so_hbm,
    bn, ne, wo, mo, so, sem,
):
    op, ip = op_ref[...], ip_ref[...]
    copies = []

    def out(src, dst):
        cp = pltpu.make_async_copy(src, dst, sem.at[len(copies)])
        cp.start()
        copies.append(cp)

    parts = []
    for j in range(8):
        half, k = j // 4, 4 * (j % 4)
        pieces = [tb_ref[n : n + 2, half].reshape(RANK, 128) for n in (k, k + 2)]
        hi, lo = split2(jnp.concatenate(pieces, axis=1))
        right = dot(ip, jnp.concatenate([hi, lo, hi], axis=0))
        bn[:, 256 * j : 256 * j + 256] = right
        hi, lo = split2(right)
        parts.append(jnp.concatenate([hi, lo, hi], axis=0))
    out(bn, bo_hbm)
    for j in range(8):
        cols = slice(256 * j, 256 * j + 256)
        approx = dot(op, parts[j])
        merged = g_ref[:, cols].astype(f32) + e_ref[:, cols].astype(f32)
        ne[:, cols] = (merged - approx[0:HID]).astype(bf16)
        out(ne.at[:, cols], ne_hbm.at[0, :, cols])
        update = approx[HID : HID + 16]
        moment_next = beta_first * m_ref[:, cols] + (1.0 - beta_first) * update
        second_next = beta_second * s_ref[:, cols] + (1.0 - beta_second) * update * update
        mo[:, cols] = moment_next
        so[:, cols] = second_next
        wo[:, cols] = w_ref[:, cols] - step_size * (moment_next / corr_first) / (
            jnp.sqrt(second_next / corr_second) + adam_eps
        )
    out(mo, mo_hbm)
    out(so, so_hbm)
    out(wo, wo_hbm)
    for cp in copies:
        cp.wait()


def apply(tb, op, ip, g, e, w, m, s):
    vm = pl.BlockSpec(memory_space=VMEM)
    rows = jax.ShapeDtypeStruct(w.shape, f32)
    return pl.pallas_call(
        apply_kernel,
        name="apply",
        out_shape=(
            jax.ShapeDtypeStruct((1, HID, D), bf16),
            jax.ShapeDtypeStruct((RANK, D), f32),
            rows, rows, rows,
        ),
        in_specs=[vm] * 8,
        out_specs=(pl.BlockSpec(memory_space=pltpu.HBM),) * 5,
        scratch_shapes=[VMEM((RANK, D), f32), VMEM((HID, D), bf16)] + [VMEM(w.shape, f32)] * 3 + [pltpu.SemaphoreType.DMA((12,))],
        compiler_params=pltpu.CompilerParams(vmem_limit_bytes=24 << 20),
    )(tb, op, ip, g, e, w, m, s)


def body(grads, errors, basis, weight, moment, second):
    tb, op, ip, g, e = exchange(grads, errors, basis.T)
    new_errors, bo, w, m, s = apply(tb, op, ip, g, e, weight, moment, second)
    return new_errors, bo.T, w, m, s


def solution(mesh):
    placed = (
        P("dp", "tensor", None),
        P("dp", "tensor", None),
        P(),
        P(("tensor", "dp"), None),
        P(("tensor", "dp"), None),
        P(("tensor", "dp"), None),
    )
    return jax.shard_map(
        body,
        mesh=mesh,
        in_specs=placed,
        out_specs=(
            P("dp", "tensor", None),
            P(),
            P(("tensor", "dp"), None),
            P(("tensor", "dp"), None),
            P(("tensor", "dp"), None),
        ),
        check_vma=False,
    )
```

```python
import jax
import jax.numpy as jnp
from jax import lax
from jax.experimental import pallas as pl
from jax.experimental.pallas import tpu as pltpu
from jax.sharding import PartitionSpec as P

beta_first = 0.9
beta_second = 0.95
step_size = 0.1
adam_eps = 1e-08
corr_first = 1.0 - 0.9**10
corr_second = 1.0 - 0.95**10

MESH = pl.DeviceIdType.MESH
VMEM = pltpu.VMEM
f32, bf16 = jnp.float32, jnp.bfloat16
D, RANK, HID, HALF, WIDE = 2048, 64, 512, 256, 1024
NX, NY, NZ = 4, 4, 8
NN = (((1,), (0,)), ((), ()))
NT = (((1,), (1,)), ((), ()))
TN = (((0,), (0,)), ((), ()))
HIGH = lax.Precision.HIGHEST


def split3(v):
    hi = v.astype(bf16)
    rest = v - hi.astype(f32)
    mid = rest.astype(bf16)
    lo = (rest - mid.astype(f32)).astype(bf16)
    return hi, mid, lo


def split2(v):
    hi = v.astype(bf16)
    return hi, (v - hi.astype(f32)).astype(bf16)


def dot(a, b, dims=NN):
    return lax.dot_general(a, b, dims, preferred_element_type=f32)


def fold(v):
    return v[0:RANK] + v[RANK : 2 * RANK] + v[2 * RANK : 3 * RANK]


def sub_row(v, k):
    return jnp.broadcast_to(v[k : k + 1, :], v.shape)


def inverse_factor(a):
    blocks = [a[8 * v : 8 * v + 8] for v in range(8)]
    sub = lax.broadcasted_iota(jnp.int32, (8, 2 * RANK), 0)
    lane = lax.broadcasted_iota(jnp.int32, (8, 2 * RANK), 1)
    for v in range(8):
        cols = {
            u: [jnp.broadcast_to(blocks[u][:, 8 * v + j : 8 * v + j + 1], (8, 2 * RANK)) for j in range(8)]
            for u in range(v, 8)
        }
        for k in range(8):
            over = 1.0 / sub_row(cols[v][k], k)
            later = [sub_row(cols[v][j], k) for j in range(k + 1, 8)]
            row = sub_row(blocks[v], k)
            for u in range(v, 8):
                times = cols[u][k] * over
                if u == v:
                    times = jnp.where(sub > k, times, 0.0)
                for j in range(k + 1, 8):
                    cols[u][j] = cols[u][j] - times * later[j - k - 1]
                blocks[u] = blocks[u] - times * row
    out = []
    for v in range(8):
        pivots = jnp.sum(jnp.where(lane == sub + 8 * v, blocks[v], 0.0), axis=1, keepdims=True)
        out.append(blocks[v] / lax.sqrt(pivots))
    return jnp.concatenate(out, axis=0)[:, RANK:]


def blocks_of(tb, ip, core):
    rights, parts = [], []
    for j in range(4):
        pieces = [tb[n : n + 2, core].reshape(RANK, 128) for n in (4 * j, 4 * j + 2)]
        hi, lo = split2(jnp.concatenate(pieces, axis=1))
        right = dot(ip, jnp.concatenate([hi, lo, hi], axis=0))
        hi, lo = split2(right)
        rights.append(right)
        parts.append(jnp.concatenate([hi, lo, hi], axis=0))
    return rights, parts


FAR = ((2, 2), (2, 1), (2, 3), (1, 2), (3, 2), (1, 1), (1, 3), (3, 1), (3, 3), (2, 0), (0, 2), (1, 0), (3, 0), (0, 1), (0, 3))
ZFAR = (4, 3, 5, 2, 6, 1, 7)


def exchange_kernel(
    g_hbm, e_hbm, b_hbm, tb, op_ref, ip_ref, g, e, bn_ref, ne_ref, up_ref,
    b, p_send, p_recv, c_buf, c_t, m_send, m_recv, s_hi, s_lo, r_all, rbuf, zbuf, gbuf,
    in_sem, p_s, p_r, c_s, c_r, ms_s, ms_r, xy_s, xy_r, z_s, z_r, gr_s, gr_r, ag_s, ag_r, fw_s, fw_r,
):
    t = lax.axis_index("tensor")
    d = lax.axis_index("dp")
    x, y, c = d // 8, (d // 2) % NY, d % 2
    oc = 1 - c
    chip = x * NY + y

    def dev(tt, xx, yy, cc):
        return (tt, (xx * NY + yy) * 2 + cc)

    sib = dev(t, x, y, oc)

    def send(src, dst, ss, rs, to):
        pltpu.make_async_remote_copy(
            src_ref=src, dst_ref=dst, send_sem=ss, recv_sem=rs, device_id=to, device_id_type=MESH
        ).start()

    def got(ref, rs):
        pltpu.make_async_remote_copy(
            src_ref=ref, dst_ref=ref, send_sem=p_s, recv_sem=rs, device_id=sib, device_id_type=MESH
        ).wait_recv()

    def sent(ref, ss):
        pltpu.make_async_remote_copy(
            src_ref=ref, dst_ref=ref, send_sem=ss, recv_sem=p_r, device_id=sib, device_id_type=MESH
        ).wait_send()

    barrier = pltpu.get_barrier_semaphore()

    def greet(to):
        pl.semaphore_signal(barrier, inc=1, device_id=to, device_id_type=MESH)

    b_in = pltpu.make_async_copy(b_hbm, b, in_sem.at[0])
    b_in.start()
    x_far = (x + 2) % NX
    x_near = x + 1 - 2 * (x % 2)
    x_mid = x_far + 1 - 2 * (x_far % 2)
    halves = (x_far // 2, x // 2)
    loads = []
    for i, half in enumerate(halves):
        for j, (src, dst) in enumerate(((g_hbm, g), (e_hbm, e))):
            for k in range(2):
                rows = pl.ds(pl.multiple_of(half * HALF + 128 * k, 128), 128)
                cp = pltpu.make_async_copy(src.at[0, rows], dst.at[rows], in_sem.at[1 + 4 * i + 2 * j + k])
                cp.start()
                loads.append(cp)
        if i == 0:
            for dz in ZFAR:
                greet(dev((t + dz) % NZ, x, y, c))
            for dx, dy in FAR:
                for cc in (c, oc):
                    greet(dev(t, (x + dx) % NX, (y + dy) % NY, cc))
            greet(sib)

    b_in.wait()
    bs = jnp.concatenate(split3(b[...]), axis=0)
    for i, half in enumerate(halves):
        rows = pl.ds(pl.multiple_of(half * HALF, HALF), HALF)
        loads[4 * i].wait()
        loads[4 * i + 1].wait()
        acc = dot(bs, g[rows, :], NT)
        loads[4 * i + 2].wait()
        loads[4 * i + 3].wait()
        part = fold(acc + dot(bs, e[rows, :], NT))
        for j in range(2):
            for k in range(8):
                p_send[16 * half + 8 * j + k] = part[8 * k : 8 * k + 8, 128 * j : 128 * j + 128]
        if i == 0:
            pl.semaphore_wait(barrier, 38)
        for xx in ((x_far, x_mid), (x_near, x))[i]:
            for dy in (2, 1, 3, 0):
                yy = (y + dy) % NY
                for cc in (oc, c):
                    n = (xx * NY + yy) * 2 + cc
                    if xx is x and dy == 0 and cc is c:
                        p_recv[n] = p_send[n]
                    else:
                        send(p_send.at[n], p_recv.at[d], p_s, p_r, dev(t, xx, yy, cc))
    theirs = pl.ds(pl.multiple_of(oc * WIDE, WIDE), WIDE)
    ours = pl.ds(pl.multiple_of(c * WIDE, WIDE), WIDE)
    for k in range(4):
        rows = pl.ds(128 * k, 128)
        m_send[rows, :] = g[rows, theirs].astype(f32) + e[rows, theirs].astype(f32)
        send(m_send.at[rows], m_recv.at[rows], ms_s.at[k], ms_r.at[k], sib)
    got(p_recv.at[pl.ds(0, 31)], p_r)
    total = p_recv[0]
    for n in range(1, 32):
        total = total + p_recv[n]
    c_buf[d] = total
    for dx, dy in FAR + ((0, 0),):
        for cc in (oc, c):
            if not (dx == 0 and dy == 0 and cc is c):
                send(c_buf.at[d], c_buf.at[d], c_s, c_r, dev(t, (x + dx) % NX, (y + dy) % NY, cc))
    for k in range(4):
        rows = pl.ds(128 * k, 128)
        got(m_recv.at[rows], ms_r.at[k])
        pair = (g[rows, ours].astype(f32) + e[rows, ours].astype(f32)) + m_recv[rows, :]
        s_hi[rows, :], s_lo[rows, :] = split2(pair)
    got(c_buf.at[pl.ds(0, 31)], c_r)
    for j in range(4):
        c_t[:, 128 * j : 128 * j + 128] = c_buf[8 * j : 8 * j + 8].reshape(RANK, 128)

    cs = jnp.concatenate(split3(c_t[...]), axis=0)

    for dx in (2, 0, 1, 3):
        xx = (x + dx) % NX
        cols = pl.ds(pl.multiple_of(xx * 256, 256), 256)
        r = fold(dot(cs, s_hi[:, cols]) + dot(cs, s_lo[:, cols]))
        for yy in range(NY):
            half, blk = yy % 2, yy // 2
            r_all[xx * NY + yy] = r[32 * half : 32 * half + 32, 128 * blk : 128 * blk + 128]
        for dy in (2, 1, 3, 0):
            yy = (y + dy) % NY
            n = xx * NY + yy
            if dx or dy:
                send(r_all.at[n], rbuf.at[chip], xy_s, xy_r, dev(t, xx, yy, c))
            else:
                rbuf[chip] = r_all[chip]
    gram = lax.dot_general(c_t[...], c_t[...], NT, precision=HIGH, preferred_element_type=f32)
    gbuf[t] = jnp.concatenate([gram[0:32], gram[32:64]], axis=1)
    for dz in ZFAR:
        send(gbuf.at[t], gbuf.at[t], gr_s, gr_r, dev((t + dz) % NZ, x, y, c))

    got(rbuf.at[pl.ds(0, 15)], xy_r)
    total = rbuf[0]
    for n in range(1, 16):
        total = total + rbuf[n]
    zbuf[t] = total
    for dz in ZFAR:
        send(zbuf.at[t], zbuf.at[t], z_s, z_r, dev((t + dz) % NZ, x, y, c))

    got(gbuf.at[pl.ds(0, 7)], gr_r)
    packed = gbuf[0]
    for n in range(1, NZ):
        packed = packed + gbuf[n]
    rows = lax.broadcasted_iota(jnp.int32, (RANK, RANK), 0)
    lanes = lax.broadcasted_iota(jnp.int32, (RANK, RANK), 1)
    gram = jnp.concatenate([packed[:, 0:64], packed[:, 64:128]], axis=0)
    a = jnp.concatenate([gram, jnp.where(rows == lanes, 1.0, 0.0)], axis=1)
    inv = inverse_factor(a)
    o_t = lax.dot_general(inv, c_t[...], NN, precision=HIGH, preferred_element_type=f32)
    o_hi, o_lo = split2(o_t.T)
    op_ref[0:HID, :] = jnp.concatenate([o_hi, o_hi, o_lo], axis=1)
    op_ref[HID : HID + 16, :] = op_ref[pl.ds(pl.multiple_of(d * 16, 16), 16), :]
    i_hi, i_lo = split2(inv * (1.0 / 32.0))
    ip_ref[...] = jnp.concatenate([i_hi, i_hi, i_lo], axis=1)

    got(zbuf.at[pl.ds(0, 7)], z_r)
    total = zbuf[0]
    for n in range(1, NZ):
        total = total + zbuf[n]
    tb[chip, c] = total
    for dx, dy in FAR:
        send(tb.at[chip, c], tb.at[chip, c], ag_s, ag_r.at[chip], dev(t, (x + dx) % NX, (y + dy) % NY, c))
    send(tb.at[chip, c], tb.at[chip, c], fw_s, fw_r.at[chip], sib)

    for dx, dy in FAR:
        n = ((x + dx) % NX) * NY + (y + dy) % NY
        got(tb.at[n, c], ag_r.at[n])
        send(tb.at[n, c], tb.at[n, c], fw_s, fw_r.at[n], sib)
    rights, parts = blocks_of(tb, ip_ref[...], c)
    for j in range(4):
        here = slice(256 * j, 256 * j + 256)
        cols = pl.ds(pl.multiple_of(c * WIDE + 256 * j, 256), 256)
        bn_ref[:, here] = rights[j]
        approx = dot(op_ref[...], parts[j])
        ne_ref[:, here] = (g[:, cols].astype(f32) + e[:, cols].astype(f32) - approx[0:HID]).astype(bf16)
        up_ref[:, here] = approx[HID : HID + 16]
    for dx, dy in ((0, 0),) + FAR:
        n = ((x + dx) % NX) * NY + (y + dy) % NY
        got(tb.at[n, oc], fw_r.at[n])

    sent(p_recv.at[pl.ds(0, 31)], p_s)
    sent(p_recv.at[pl.ds(0, 31)], c_s)
    for k in range(4):
        sent(m_recv.at[pl.ds(128 * k, 128)], ms_s.at[k])
    sent(rbuf.at[pl.ds(0, 15)], xy_s)
    sent(zbuf.at[pl.ds(0, 7)], z_s)
    sent(gbuf.at[pl.ds(0, 7)], gr_s)
    sent(rbuf.at[pl.ds(0, 15)], ag_s)
    sent(rbuf, fw_s)


def exchange(g, e, b_t):
    hbm = pl.BlockSpec(memory_space=pltpu.HBM)
    vm = pl.BlockSpec(memory_space=VMEM)
    dma = pltpu.SemaphoreType.DMA
    return pl.pallas_call(
        exchange_kernel,
        name="exchange",
        out_shape=(
            jax.ShapeDtypeStruct((16, 2, 32, 128), f32),
            jax.ShapeDtypeStruct((HID + 16, 3 * RANK), bf16),
            jax.ShapeDtypeStruct((RANK, 3 * RANK), bf16),
            jax.ShapeDtypeStruct((HID, D), bf16),
            jax.ShapeDtypeStruct((HID, D), bf16),
            jax.ShapeDtypeStruct((RANK, WIDE), f32),
            jax.ShapeDtypeStruct((HID, WIDE), bf16),
            jax.ShapeDtypeStruct((16, WIDE), f32),
        ),
        in_specs=[hbm] * 3,
        out_specs=(vm,) * 8,
        scratch_shapes=[
            VMEM((RANK, D), f32),
            VMEM((32, 8, 128), f32),
            VMEM((32, 8, 128), f32),
            VMEM((32, 8, 128), f32),
            VMEM((RANK, HID), f32),
            VMEM((HID, WIDE), f32),
            VMEM((HID, WIDE), f32),
            VMEM((HID, WIDE), bf16),
            VMEM((HID, WIDE), bf16),
            VMEM((16, 32, 128), f32),
            VMEM((16, 32, 128), f32),
            VMEM((NZ, 32, 128), f32),
            VMEM((NZ, 32, 128), f32),
            dma((9,)),
            dma, dma, dma, dma,
            dma((4,)), dma((4,)),
            dma, dma, dma, dma, dma, dma,
            dma, dma((16,)), dma, dma((16,)),
        ],
        compiler_params=pltpu.CompilerParams(
            collective_id=0, has_side_effects=True, vmem_limit_bytes=24 << 20
        ),
    )(*(pltpu.with_memory_space_constraint(v, pltpu.HBM) for v in (g, e, b_t)))


def apply_kernel(
    tb_ref, op_ref, ip_ref, g_ref, e_ref, bn_ref, ne_ref, up_ref, w_ref, m_ref, s_ref,
    ne_hbm, bo_hbm, wo_hbm, mo_hbm, so_hbm, bn, ne, wo, mo, so, sem,
):
    c = lax.axis_index("dp") % 2
    oc = 1 - c
    copies = []

    def out(src, dst):
        cp = pltpu.make_async_copy(src, dst, sem.at[len(copies)])
        cp.start()
        copies.append(cp)

    def span(half, start, size):
        return pl.ds(pl.multiple_of(half * WIDE + start, size), size)

    def adam(cols, update):
        moment_next = beta_first * m_ref[:, cols] + (1.0 - beta_first) * update
        second_next = beta_second * s_ref[:, cols] + (1.0 - beta_second) * update * update
        mo[:, cols] = moment_next
        so[:, cols] = second_next
        wo[:, cols] = w_ref[:, cols] - step_size * (moment_next / corr_first) / (
            jnp.sqrt(second_next / corr_second) + adam_eps
        )

    for j in range(2):
        here = pl.ds(512 * j, 512)
        out(ne_ref.at[:, here], ne_hbm.at[0, :, span(c, 512 * j, 512)])
    out(bn_ref, bo_hbm.at[:, span(c, 0, WIDE)])
    rights, parts = blocks_of(tb_ref, ip_ref[...], oc)
    for j in range(4):
        bn[:, 256 * j : 256 * j + 256] = rights[j]
    out(bn, bo_hbm.at[:, span(oc, 0, WIDE)])
    op = op_ref[...]
    for j in range(4):
        here = slice(256 * j, 256 * j + 256)
        cols = span(oc, 256 * j, 256)
        approx = dot(op, parts[j])
        ne[:, here] = (g_ref[:, cols].astype(f32) + e_ref[:, cols].astype(f32) - approx[0:HID]).astype(bf16)
        out(ne.at[:, here], ne_hbm.at[0, :, cols])
        adam(cols, approx[HID : HID + 16])
        adam(span(c, 256 * j, 256), up_ref[:, here])
    out(mo, mo_hbm)
    out(so, so_hbm)
    out(wo, wo_hbm)
    for cp in copies:
        cp.wait()


def apply(tb, op, ip, g, e, bn, ne, up, w, m, s):
    vm = pl.BlockSpec(memory_space=VMEM)
    rows = jax.ShapeDtypeStruct(w.shape, f32)
    return pl.pallas_call(
        apply_kernel,
        name="apply",
        out_shape=(
            jax.ShapeDtypeStruct((1, HID, D), bf16),
            jax.ShapeDtypeStruct((RANK, D), f32),
            rows, rows, rows,
        ),
        in_specs=[vm] * 11,
        out_specs=(pl.BlockSpec(memory_space=pltpu.HBM),) * 5,
        scratch_shapes=[VMEM((RANK, WIDE), f32), VMEM((HID, WIDE), bf16)] + [VMEM(w.shape, f32)] * 3 + [pltpu.SemaphoreType.DMA((12,))],
        compiler_params=pltpu.CompilerParams(vmem_limit_bytes=24 << 20),
    )(tb, op, ip, g, e, bn, ne, up, w, m, s)


def body(grads, errors, basis, weight, moment, second):
    parts = exchange(grads, errors, basis.T)
    new_errors, bo, w, m, s = apply(*parts, weight, moment, second)
    return new_errors, bo.T, w, m, s


def solution(mesh):
    placed = (
        P("dp", "tensor", None),
        P("dp", "tensor", None),
        P(),
        P(("tensor", "dp"), None),
        P(("tensor", "dp"), None),
        P(("tensor", "dp"), None),
    )
    return jax.shard_map(
        body,
        mesh=mesh,
        in_specs=placed,
        out_specs=(
            P("dp", "tensor", None),
            P(),
            P(("tensor", "dp"), None),
            P(("tensor", "dp"), None),
            P(("tensor", "dp"), None),
        ),
        check_vma=False,
    )
```

```python
import jax
import jax.numpy as jnp
from jax import lax
from jax.experimental import pallas as pl
from jax.experimental.pallas import tpu as pltpu
from jax.sharding import PartitionSpec as P

beta_first = 0.9
beta_second = 0.95
step_size = 0.1
adam_eps = 1e-08
corr_first = 1.0 - 0.9**10
corr_second = 1.0 - 0.95**10

MESH = pl.DeviceIdType.MESH
VMEM = pltpu.VMEM
f32, bf16 = jnp.float32, jnp.bfloat16
D, RANK, HID, HALF, WIDE = 2048, 64, 512, 256, 1024
NX, NY, NZ = 4, 4, 8
NN = (((1,), (0,)), ((), ()))
NT = (((1,), (1,)), ((), ()))
TN = (((0,), (0,)), ((), ()))
HIGH = lax.Precision.HIGHEST


def split3(v):
    hi = v.astype(bf16)
    rest = v - hi.astype(f32)
    mid = rest.astype(bf16)
    lo = (rest - mid.astype(f32)).astype(bf16)
    return hi, mid, lo


def split2(v):
    hi = v.astype(bf16)
    return hi, (v - hi.astype(f32)).astype(bf16)


def dot(a, b, dims=NN):
    return lax.dot_general(a, b, dims, preferred_element_type=f32)


def fold(v):
    return v[0:RANK] + v[RANK : 2 * RANK] + v[2 * RANK : 3 * RANK]


def sub_row(v, k):
    return jnp.broadcast_to(v[k : k + 1, :], v.shape)


def inverse_factor(a):
    blocks = [a[8 * v : 8 * v + 8] for v in range(8)]
    sub = lax.broadcasted_iota(jnp.int32, (8, 2 * RANK), 0)
    lane = lax.broadcasted_iota(jnp.int32, (8, 2 * RANK), 1)
    for v in range(8):
        cols = {
            u: [jnp.broadcast_to(blocks[u][:, 8 * v + j : 8 * v + j + 1], (8, 2 * RANK)) for j in range(8)]
            for u in range(v, 8)
        }
        for k in range(8):
            over = 1.0 / sub_row(cols[v][k], k)
            later = [sub_row(cols[v][j], k) for j in range(k + 1, 8)]
            row = sub_row(blocks[v], k)
            for u in range(v, 8):
                times = cols[u][k] * over
                if u == v:
                    times = jnp.where(sub > k, times, 0.0)
                for j in range(k + 1, 8):
                    cols[u][j] = cols[u][j] - times * later[j - k - 1]
                blocks[u] = blocks[u] - times * row
    out = []
    for v in range(8):
        pivots = jnp.sum(jnp.where(lane == sub + 8 * v, blocks[v], 0.0), axis=1, keepdims=True)
        out.append(blocks[v] / lax.sqrt(pivots))
    return jnp.concatenate(out, axis=0)[:, RANK:]


def blocks_of(tb, ip, core):
    rights, parts = [], []
    for j in range(4):
        pieces = [tb[n : n + 2, core].reshape(RANK, 128) for n in (4 * j, 4 * j + 2)]
        hi, lo = split2(jnp.concatenate(pieces, axis=1))
        right = dot(ip, jnp.concatenate([hi, lo, hi], axis=0))
        hi, lo = split2(right)
        rights.append(right)
        parts.append(jnp.concatenate([hi, lo, hi], axis=0))
    return rights, parts


FAR = ((2, 2), (2, 1), (2, 3), (1, 2), (3, 2), (1, 1), (1, 3), (3, 1), (3, 3), (2, 0), (0, 2), (1, 0), (3, 0), (0, 1), (0, 3))
ZFAR = (4, 3, 5, 2, 6, 1, 7)


def exchange_kernel(
    g_hbm, e_hbm, b_hbm, tb, op_ref, ip_ref, g, e, bn_ref, ne_ref, up_ref,
    b, p_send, p_recv, c_buf, c_t, m_send, m_recv, s_hi, s_lo, r_all, rbuf, zbuf, gbuf,
    in_sem, p_s, p_r, c_s, c_r, ms_s, ms_r, xy_s, xy_r, z_s, z_r, gr_s, gr_r, ag_s, ag_r, fw_s, fw_r,
):
    t = lax.axis_index("tensor")
    d = lax.axis_index("dp")
    x, y, c = d // 8, (d // 2) % NY, d % 2
    oc = 1 - c
    chip = x * NY + y

    def dev(tt, xx, yy, cc):
        return (tt, (xx * NY + yy) * 2 + cc)

    sib = dev(t, x, y, oc)

    def send(src, dst, ss, rs, to):
        pltpu.make_async_remote_copy(
            src_ref=src, dst_ref=dst, send_sem=ss, recv_sem=rs, device_id=to, device_id_type=MESH
        ).start()

    def got(ref, rs):
        pltpu.make_async_remote_copy(
            src_ref=ref, dst_ref=ref, send_sem=p_s, recv_sem=rs, device_id=sib, device_id_type=MESH
        ).wait_recv()

    def sent(ref, ss):
        pltpu.make_async_remote_copy(
            src_ref=ref, dst_ref=ref, send_sem=ss, recv_sem=p_r, device_id=sib, device_id_type=MESH
        ).wait_send()

    barrier = pltpu.get_barrier_semaphore()

    def greet(to):
        pl.semaphore_signal(barrier, inc=1, device_id=to, device_id_type=MESH)

    b_in = []
    for k in range(4):
        some = pl.ds(16 * k, 16)
        b_in.append(pltpu.make_async_copy(b_hbm.at[some], b.at[some], in_sem.at[8 + k]))
        b_in[k].start()
    x_far = (x + 2) % NX
    x_near = x + 1 - 2 * (x % 2)
    x_mid = x_far + 1 - 2 * (x_far % 2)
    halves = (x_far // 2, x // 2)
    loads = []
    for i, half in enumerate(halves):
        for j, (src, dst) in enumerate(((g_hbm, g), (e_hbm, e))):
            for k in range(2):
                rows = pl.ds(pl.multiple_of(half * HALF + 128 * k, 128), 128)
                cp = pltpu.make_async_copy(src.at[0, rows], dst.at[rows], in_sem.at[4 * i + 2 * j + k])
                cp.start()
                loads.append(cp)
        if i == 0:
            for dz in ZFAR:
                greet(dev((t + dz) % NZ, x, y, c))
            for dx, dy in FAR:
                for cc in (c, oc):
                    greet(dev(t, (x + dx) % NX, (y + dy) % NY, cc))
            greet(sib)

    for cp in b_in:
        cp.wait()
    bs = jnp.concatenate(split3(b[...]), axis=0)
    for i, half in enumerate(halves):
        rows = pl.ds(pl.multiple_of(half * HALF, HALF), HALF)
        loads[4 * i].wait()
        loads[4 * i + 1].wait()
        acc = dot(bs, g[rows, :], NT)
        loads[4 * i + 2].wait()
        loads[4 * i + 3].wait()
        part = fold(acc + dot(bs, e[rows, :], NT))
        for j in range(2):
            for k in range(8):
                p_send[16 * half + 8 * j + k] = part[8 * k : 8 * k + 8, 128 * j : 128 * j + 128]
        if i == 0:
            pl.semaphore_wait(barrier, 38)
        for xx in ((x_far, x_mid), (x_near, x))[i]:
            for dy in (2, 1, 3, 0):
                yy = (y + dy) % NY
                for cc in (oc, c):
                    n = (xx * NY + yy) * 2 + cc
                    if xx is x and dy == 0 and cc is c:
                        p_recv[n] = p_send[n]
                    else:
                        send(p_send.at[n], p_recv.at[d], p_s, p_r, dev(t, xx, yy, cc))
    theirs = pl.ds(pl.multiple_of(oc * WIDE, WIDE), WIDE)
    ours = pl.ds(pl.multiple_of(c * WIDE, WIDE), WIDE)
    for k in range(4):
        rows = pl.ds(128 * k, 128)
        m_send[rows, :] = g[rows, theirs].astype(f32) + e[rows, theirs].astype(f32)
        send(m_send.at[rows], m_recv.at[rows], ms_s.at[k], ms_r.at[k], sib)
    got(p_recv.at[pl.ds(0, 31)], p_r)
    total = p_recv[0]
    for n in range(1, 32):
        total = total + p_recv[n]
    c_buf[d] = total
    for dx, dy in FAR + ((0, 0),):
        for cc in (oc, c):
            if not (dx == 0 and dy == 0 and cc is c):
                send(c_buf.at[d], c_buf.at[d], c_s, c_r, dev(t, (x + dx) % NX, (y + dy) % NY, cc))
    for k in range(4):
        rows = pl.ds(128 * k, 128)
        got(m_recv.at[rows], ms_r.at[k])
        pair = (g[rows, ours].astype(f32) + e[rows, ours].astype(f32)) + m_recv[rows, :]
        s_hi[rows, :], s_lo[rows, :] = split2(pair)
    got(c_buf.at[pl.ds(0, 31)], c_r)
    for j in range(4):
        c_t[:, 128 * j : 128 * j + 128] = c_buf[8 * j : 8 * j + 8].reshape(RANK, 128)

    cs = jnp.concatenate(split3(c_t[...]), axis=0)

    for dx in (2, 0, 1, 3):
        xx = (x + dx) % NX
        cols = pl.ds(pl.multiple_of(xx * 256, 256), 256)
        r = fold(dot(cs, s_hi[:, cols]) + dot(cs, s_lo[:, cols]))
        for yy in range(NY):
            half, blk = yy % 2, yy // 2
            r_all[xx * NY + yy] = r[32 * half : 32 * half + 32, 128 * blk : 128 * blk + 128]
        for dy in (2, 1, 3, 0):
            yy = (y + dy) % NY
            n = xx * NY + yy
            if dx or dy:
                send(r_all.at[n], rbuf.at[chip], xy_s, xy_r, dev(t, xx, yy, c))
            else:
                rbuf[chip] = r_all[chip]
    gram = lax.dot_general(c_t[...], c_t[...], NT, precision=HIGH, preferred_element_type=f32)
    gbuf[t] = jnp.concatenate([gram[0:32], gram[32:64]], axis=1)
    for dz in ZFAR:
        send(gbuf.at[t], gbuf.at[t], gr_s, gr_r, dev((t + dz) % NZ, x, y, c))

    got(rbuf.at[pl.ds(0, 15)], xy_r)
    total = rbuf[0]
    for n in range(1, 16):
        total = total + rbuf[n]
    zbuf[t] = total
    for dz in ZFAR:
        send(zbuf.at[t], zbuf.at[t], z_s, z_r, dev((t + dz) % NZ, x, y, c))

    got(gbuf.at[pl.ds(0, 7)], gr_r)
    packed = gbuf[0]
    for n in range(1, NZ):
        packed = packed + gbuf[n]
    rows = lax.broadcasted_iota(jnp.int32, (RANK, RANK), 0)
    lanes = lax.broadcasted_iota(jnp.int32, (RANK, RANK), 1)
    gram = jnp.concatenate([packed[:, 0:64], packed[:, 64:128]], axis=0)
    a = jnp.concatenate([gram, jnp.where(rows == lanes, 1.0, 0.0)], axis=1)
    inv = inverse_factor(a)
    o_t = lax.dot_general(inv, c_t[...], NN, precision=HIGH, preferred_element_type=f32)
    o_hi, o_lo = split2(o_t.T)
    op_ref[0:HID, :] = jnp.concatenate([o_hi, o_hi, o_lo], axis=1)
    op_ref[HID : HID + 16, :] = op_ref[pl.ds(pl.multiple_of(d * 16, 16), 16), :]
    i_hi, i_lo = split2(inv * (1.0 / 32.0))
    ip_ref[...] = jnp.concatenate([i_hi, i_hi, i_lo], axis=1)

    got(zbuf.at[pl.ds(0, 7)], z_r)
    total = zbuf[0]
    for n in range(1, NZ):
        total = total + zbuf[n]
    tb[chip, c] = total
    for dx, dy in FAR:
        send(tb.at[chip, c], tb.at[chip, c], ag_s, ag_r.at[chip], dev(t, (x + dx) % NX, (y + dy) % NY, c))
    send(tb.at[chip, c], tb.at[chip, c], fw_s, fw_r.at[chip], sib)

    for dx, dy in FAR:
        n = ((x + dx) % NX) * NY + (y + dy) % NY
        got(tb.at[n, c], ag_r.at[n])
        send(tb.at[n, c], tb.at[n, c], fw_s, fw_r.at[n], sib)
    rights, parts = blocks_of(tb, ip_ref[...], c)
    for j in range(4):
        here = slice(256 * j, 256 * j + 256)
        cols = pl.ds(pl.multiple_of(c * WIDE + 256 * j, 256), 256)
        bn_ref[:, here] = rights[j]
        approx = dot(op_ref[...], parts[j])
        ne_ref[:, here] = (g[:, cols].astype(f32) + e[:, cols].astype(f32) - approx[0:HID]).astype(bf16)
        up_ref[:, here] = approx[HID : HID + 16]
    for dx, dy in ((0, 0),) + FAR:
        n = ((x + dx) % NX) * NY + (y + dy) % NY
        got(tb.at[n, oc], fw_r.at[n])

    sent(p_recv.at[pl.ds(0, 31)], p_s)
    sent(p_recv.at[pl.ds(0, 31)], c_s)
    for k in range(4):
        sent(m_recv.at[pl.ds(128 * k, 128)], ms_s.at[k])
    sent(rbuf.at[pl.ds(0, 15)], xy_s)
    sent(zbuf.at[pl.ds(0, 7)], z_s)
    sent(gbuf.at[pl.ds(0, 7)], gr_s)
    sent(rbuf.at[pl.ds(0, 15)], ag_s)
    sent(rbuf, fw_s)


def exchange(g, e, b_t):
    hbm = pl.BlockSpec(memory_space=pltpu.HBM)
    vm = pl.BlockSpec(memory_space=VMEM)
    dma = pltpu.SemaphoreType.DMA
    return pl.pallas_call(
        exchange_kernel,
        name="exchange",
        out_shape=(
            jax.ShapeDtypeStruct((16, 2, 32, 128), f32),
            jax.ShapeDtypeStruct((HID + 16, 3 * RANK), bf16),
            jax.ShapeDtypeStruct((RANK, 3 * RANK), bf16),
            jax.ShapeDtypeStruct((HID, D), bf16),
            jax.ShapeDtypeStruct((HID, D), bf16),
            jax.ShapeDtypeStruct((RANK, WIDE), f32),
            jax.ShapeDtypeStruct((HID, WIDE), bf16),
            jax.ShapeDtypeStruct((16, WIDE), f32),
        ),
        in_specs=[hbm] * 3,
        out_specs=(vm,) * 8,
        scratch_shapes=[
            VMEM((RANK, D), f32),
            VMEM((32, 8, 128), f32),
            VMEM((32, 8, 128), f32),
            VMEM((32, 8, 128), f32),
            VMEM((RANK, HID), f32),
            VMEM((HID, WIDE), f32),
            VMEM((HID, WIDE), f32),
            VMEM((HID, WIDE), bf16),
            VMEM((HID, WIDE), bf16),
            VMEM((16, 32, 128), f32),
            VMEM((16, 32, 128), f32),
            VMEM((NZ, 32, 128), f32),
            VMEM((NZ, 32, 128), f32),
            dma((12,)),
            dma, dma, dma, dma,
            dma((4,)), dma((4,)),
            dma, dma, dma, dma, dma, dma,
            dma, dma((16,)), dma, dma((16,)),
        ],
        compiler_params=pltpu.CompilerParams(
            collective_id=0, has_side_effects=True, vmem_limit_bytes=24 << 20
        ),
    )(*(pltpu.with_memory_space_constraint(v, pltpu.HBM) for v in (g, e, b_t)))


def apply_kernel(
    tb_ref, op_ref, ip_ref, g_ref, e_ref, bn_ref, ne_ref, up_ref, w_ref, m_ref, s_ref,
    ne_hbm, bo_hbm, wo_hbm, mo_hbm, so_hbm, bn, ne, wo, mo, so, sem,
):
    c = lax.axis_index("dp") % 2
    oc = 1 - c
    copies = []

    def out(src, dst):
        cp = pltpu.make_async_copy(src, dst, sem.at[len(copies)])
        cp.start()
        copies.append(cp)

    def span(half, start, size):
        return pl.ds(pl.multiple_of(half * WIDE + start, size), size)

    def adam(cols, update):
        moment_next = beta_first * m_ref[:, cols] + (1.0 - beta_first) * update
        second_next = beta_second * s_ref[:, cols] + (1.0 - beta_second) * update * update
        mo[:, cols] = moment_next
        so[:, cols] = second_next
        wo[:, cols] = w_ref[:, cols] - step_size * (moment_next / corr_first) / (
            jnp.sqrt(second_next / corr_second) + adam_eps
        )

    for j in range(2):
        here = pl.ds(512 * j, 512)
        out(ne_ref.at[:, here], ne_hbm.at[0, :, span(c, 512 * j, 512)])
    out(bn_ref, bo_hbm.at[:, span(c, 0, WIDE)])
    rights, parts = blocks_of(tb_ref, ip_ref[...], oc)
    for j in range(4):
        bn[:, 256 * j : 256 * j + 256] = rights[j]
    out(bn, bo_hbm.at[:, span(oc, 0, WIDE)])
    op = op_ref[...]
    for j in range(4):
        here = slice(256 * j, 256 * j + 256)
        cols = span(oc, 256 * j, 256)
        approx = dot(op, parts[j])
        ne[:, here] = (g_ref[:, cols].astype(f32) + e_ref[:, cols].astype(f32) - approx[0:HID]).astype(bf16)
        out(ne.at[:, here], ne_hbm.at[0, :, cols])
        adam(cols, approx[HID : HID + 16])
        adam(span(c, 256 * j, 256), up_ref[:, here])
    out(mo, mo_hbm)
    out(so, so_hbm)
    out(wo, wo_hbm)
    for cp in copies:
        cp.wait()


def apply(tb, op, ip, g, e, bn, ne, up, w, m, s):
    vm = pl.BlockSpec(memory_space=VMEM)
    rows = jax.ShapeDtypeStruct(w.shape, f32)
    return pl.pallas_call(
        apply_kernel,
        name="apply",
        out_shape=(
            jax.ShapeDtypeStruct((1, HID, D), bf16),
            jax.ShapeDtypeStruct((RANK, D), f32),
            rows, rows, rows,
        ),
        in_specs=[vm] * 11,
        out_specs=(pl.BlockSpec(memory_space=pltpu.HBM),) * 5,
        scratch_shapes=[VMEM((RANK, WIDE), f32), VMEM((HID, WIDE), bf16)] + [VMEM(w.shape, f32)] * 3 + [pltpu.SemaphoreType.DMA((12,))],
        compiler_params=pltpu.CompilerParams(vmem_limit_bytes=24 << 20),
    )(tb, op, ip, g, e, bn, ne, up, w, m, s)


def body(grads, errors, basis, weight, moment, second):
    parts = exchange(grads, errors, basis.T)
    new_errors, bo, w, m, s = apply(*parts, weight, moment, second)
    return new_errors, bo.T, w, m, s


def solution(mesh):
    placed = (
        P("dp", "tensor", None),
        P("dp", "tensor", None),
        P(),
        P(("tensor", "dp"), None),
        P(("tensor", "dp"), None),
        P(("tensor", "dp"), None),
    )
    return jax.shard_map(
        body,
        mesh=mesh,
        in_specs=placed,
        out_specs=(
            P("dp", "tensor", None),
            P(),
            P(("tensor", "dp"), None),
            P(("tensor", "dp"), None),
            P(("tensor", "dp"), None),
        ),
        check_vma=False,
    )
```
